128 devices in a mesh: pool: 2 (over y_lo), dp: 8 (over x, core), tp: 8 (over y_hi, z).
Axes of the slice: x: 4, y: 4 (y_hi: 2, y_lo: 2; y = y_hi * 2 + y_lo), z: 4, core: 2. Of those that a mesh axis runs over, the one named last changes fastest.
Arguments:
- hidden: bfloat16 [2, 8192, 8192], P('pool', 'dp', 'tp'), may hold values from -6 to 6
- w_kv: bfloat16 [8192, 2, 1024], P(None, None, 'tp'), may hold values from -0.0625 to 0.0625
- cache: bfloat16 [2, 32, 2048, 2, 1024], P('pool', 'dp', None, None, 'tp'), may hold values from -6 to 6
- query: bfloat16 [2, 32, 8192], P('pool', 'dp', 'tp'), may hold values from -80 to 80
- new_kv: bfloat16 [2, 32, 2, 1024], P('pool', 'dp', None, 'tp'), may hold values from -6 to 6
- lengths: int32 [2, 32], P('pool', 'dp'), may hold values from 1 to 2048
- assign: int32 [2, 8], replicated, may hold values from 0 to 31, as said below
Outputs:
- attended: bfloat16 [2, 32, 8192], P('pool', 'dp', 'tp')
The draws below stay inside these ranges and needn't reach their ends.
Inputs may be any that keep to these rules, and one draw needn't show every extreme that they name: `assign`: the prompts of a pool name different rows; rows 0 and 31 are always named.
All inputs are finite; a program needn't handle non-finite values.
Results may differ from the reference program's by a relative error of at most 0.0045.
Values may be sent and summed in bfloat16 or wider, within the bound.
No kernel may reach another device: no remote copies, remote signals or barrier semaphores. Data moves between devices by JAX's collectives and lax.ppermute only.
A program may use at most 128 MiB of HBM per device.

```python
import jax
import jax.numpy as jnp

D = 8192
QH = 64
KVH = 8
HD = 128
PLEN = 1024
CAP = 2048
PROMPTS = 8
ROWS = 32
PTOK = 8192


def cache_base(key):
    base = jax.random.normal(key, (2, ROWS, CAP, 2, KVH * HD), jnp.float32)
    return jnp.clip(base, -6.0, 6.0)


def draw_cache(key, part):
    return cache_base(key).astype(jnp.bfloat16)


def draw_query(key, part):
    key = jax.random.fold_in(key, 5)
    values = jnp.clip(jax.random.normal(key, (2, ROWS, QH * HD), jnp.float32), -6.0, 6.0)
    return values.astype(jnp.bfloat16)


def draw_assign(key, part):
    key = jax.random.fold_in(key, 7)
    lists = []
    for pool in range(2):
        sub = jax.random.fold_in(key, pool)
        inner = jax.random.permutation(jax.random.fold_in(sub, 1), ROWS - 2)[:PROMPTS - 2] + 1
        named = jnp.concatenate([jnp.array([0, ROWS - 1], jnp.int32), inner.astype(jnp.int32)])
        order = jax.random.permutation(jax.random.fold_in(sub, 2), PROMPTS)
        lists.append(named[order])
    return jnp.stack(lists).astype(jnp.int32)


def touch_ends(result, key, least, largest):
    dims = result.shape
    spot = [jax.random.randint(jax.random.fold_in(key, axis), (), 0, dims[axis]) for axis in range(len(dims))]
    result = result.at[tuple(spot)].set(least)
    longest = dims.index(max(dims))
    spot[longest] = (spot[longest] + 1) % dims[longest]
    return result.at[tuple(spot)].set(largest)


def block_scale(own_key, extent, shards, least, largest):
    def one(dim, shards_of):
        steps = jax.random.uniform(jax.random.fold_in(jax.random.fold_in(own_key, 6), dim), (shards_of,), jnp.float32, least / len(shards), largest / len(shards))
        return jnp.repeat(jnp.exp(steps), extent[dim] // shards_of).reshape((-1,) + (1,) * (len(extent) - dim - 1))

    gain = one(*shards[0])
    for cut in shards[1:]:
        gain = gain * one(*cut)
    return gain


def gaussian(own_key, dims, spread, limit, pieces=(), held_as=jnp.bfloat16):
    entries = jax.random.normal(own_key, dims, jnp.float32) * spread
    if len(pieces) > 0:
        entries = block_scale(own_key, dims, pieces, -0.22, 0.18) * entries
    return jnp.clip(entries, min=-limit, max=limit).astype(held_as)


def setup_inputs(seed: int = 0) -> dict:
    seeds = jax.random.split(jax.random.key(seed), 8)
    hidden = gaussian(seeds[0], (2, PTOK, D), 1.0, 6.0, ((0, 2), (1, 8), (2, 8)))
    w_kv = gaussian(seeds[1], (D, 2, KVH * HD), D ** -0.5, 0.0625, ((2, 8),))
    cache = draw_cache(jax.random.fold_in(seeds[7], 71), 0)
    query = draw_query(jax.random.fold_in(seeds[7], 71), 0)
    new_kv = gaussian(seeds[4], (2, ROWS, 2, KVH * HD), 1.0, 6.0, ((0, 2), (1, 8), (3, 8)))
    lengths = touch_ends(jax.random.randint(seeds[5], (2, ROWS), 1, CAP + 1), jax.random.fold_in(seeds[5], 1), 1, CAP).astype(jnp.int32)
    assign = draw_assign(jax.random.fold_in(seeds[7], 71), 0)
    return {"hidden": hidden, "w_kv": w_kv, "cache": cache, "query": query, "new_kv": new_kv, "lengths": lengths, "assign": assign}


def attend(query, keys_all, own, live, head):
    rows = query.shape[0]
    width = keys_all.shape[-1]
    kvd = width // head
    cap = keys_all.shape[1]
    groups = query.shape[1] // width
    q = query.reshape(rows, kvd, groups, head).astype(jnp.float32)
    k = keys_all[:, :, 0].reshape(rows, cap, kvd, head).astype(jnp.float32)
    v = keys_all[:, :, 1].reshape(rows, cap, kvd, head).astype(jnp.float32)
    own_k = own[:, 0].reshape(rows, kvd, head).astype(jnp.float32)
    own_v = own[:, 1].reshape(rows, kvd, head).astype(jnp.float32)
    scale = head ** -0.5
    scores = jnp.einsum('rkgd,rckd->rkgc', q, k) * scale
    own_score = jnp.einsum('rkgd,rkd->rkg', q, own_k) * scale
    valid = jnp.arange(cap, dtype=jnp.int32)[None, None, None, :] < live[:, None, None, None]
    masked = jnp.where(valid, scores, jnp.float32(-1e30))
    top = jnp.maximum(jnp.max(masked, axis=-1), own_score)
    weights = jnp.where(valid, jnp.exp(masked - top[..., None]), jnp.float32(0.0))
    own_weight = jnp.exp(own_score - top)
    total = jnp.sum(weights, axis=-1) + own_weight
    weights_b = weights.astype(jnp.bfloat16).astype(jnp.float32)
    own_b = own_weight.astype(jnp.bfloat16).astype(jnp.float32)
    mixed = jnp.einsum('rkgc,rckd->rkgd', weights_b, v) + own_b[..., None] * own_v[:, :, None, :]
    mixed = mixed / total[..., None]
    return mixed.reshape(rows, kvd * groups * head).astype(jnp.bfloat16)


def reference(hidden, w_kv, cache, query, new_kv, lengths, assign):
    outs = []
    for pool in range(2):
        other = 1 - pool
        flat = jnp.dot(hidden[other], w_kv.reshape(D, 2 * KVH * HD), preferred_element_type=jnp.float32)
        prompt_kv = flat.astype(jnp.bfloat16).reshape(PROMPTS, PLEN, 2, KVH * HD)
        match = assign[other][None, :] == jnp.arange(ROWS, dtype=jnp.int32)[:, None]
        taken = jnp.any(match, axis=1)
        which = jnp.sum(jnp.where(match, jnp.arange(PROMPTS, dtype=jnp.int32)[None, :], 0), axis=1).astype(jnp.int32)
        picked = prompt_kv[which]
        resident = cache[pool]
        front = jnp.where(taken[:, None, None, None], picked, resident[:, :PLEN])
        keys_all = jnp.concatenate([front, resident[:, PLEN:]], axis=1)
        live = jnp.where(taken, jnp.int32(PLEN), lengths[pool]).astype(jnp.int32)
        outs.append(attend(query[pool], keys_all, new_kv[pool], live, HD))
    return jnp.stack(outs)
```

```python
import functools

import jax
import jax.numpy as jnp
from jax import lax
from jax.experimental import pallas as pl
from jax.experimental.pallas import tpu as pltpu
from jax.sharding import PartitionSpec as P

HD = 128
F32 = jnp.float32
BF16 = jnp.bfloat16
NEG = -1e30


def nt(a, b):
    return lax.dot_general(a, b, (((1,), (1,)), ((), ())), preferred_element_type=F32)


def nn(a, b):
    return jnp.dot(a, b, preferred_element_type=F32)


def split(x):
    hi = x.astype(BF16)
    lo = (x - hi.astype(F32)).astype(BF16)
    return hi, lo


def heads_of(row, groups):
    return jnp.concatenate([row[:, h * HD:(h + 1) * HD] for h in range(groups)], axis=0)


def spread(rows, cols, odd):
    r = lax.broadcasted_iota(jnp.int32, (rows, cols), 0)
    c = lax.broadcasted_iota(jnp.int32, (rows, cols), 1)
    return jnp.where(r == 2 * c + odd, 1.0, 0.0).astype(F32).astype(BF16)


def gather_t(rows, cols, odd):
    r = lax.broadcasted_iota(jnp.int32, (rows, cols), 0)
    c = lax.broadcasted_iota(jnp.int32, (rows, cols), 1)
    return jnp.where(c == 2 * r + odd, 1.0, 0.0).astype(F32).astype(BF16)


def own_of(packed):
    q = packed[0:8]
    k = packed[8:9]
    v = packed[9:10]
    return jnp.sum(q * k, axis=1, keepdims=True) * (HD ** -0.5), v


def send_kernel(meta, assign, query, own, out):
    other, g = 1 - meta[0], meta[1]
    rows = query.shape[0]
    n = assign.shape[1]
    q = query[...].astype(F32)
    kv = own[...].astype(F32)
    packed = []
    for j in range(rows):
        mine = heads_of(q[j:j + 1], q.shape[1] // HD)
        pad = jnp.zeros((16 - mine.shape[0] - 2, HD), F32)
        packed.append(jnp.concatenate([mine, kv[2 * j:2 * j + 2], pad], axis=0))
    for i in range(n):
        at = assign[other, i] - g * rows
        value = packed[0]
        for j in range(1, rows):
            value = jnp.where(at == j, packed[j], value)
        value = value.astype(BF16)
        out[i] = value
        out[n + i] = value


def source(meta, assign):
    me, g = meta[0], meta[1]
    return (1 - me) * assign.shape[1] + assign[me, g] // meta[2]


def fold_kernel(meta, assign, got, w_low, w_high, out):
    q = got[source(meta, assign)][0:8]
    dloc = w_low.shape[0] // 2
    even = spread(256, 128, 0)
    for part, w in enumerate((w_low, w_high)):
        wide = nt(q, w[...])
        hi, lo = split(wide)
        both = jnp.concatenate([hi, lo], axis=0)
        blocks = both.shape[1] // 256
        tall = jnp.concatenate([both[:, b * 256:(b + 1) * 256] for b in range(blocks)], axis=0)
        kept = nn(tall, even)
        value = jnp.concatenate(
            [kept[b * 16:b * 16 + 8] + kept[b * 16 + 8:b * 16 + 16] for b in range(blocks)], axis=1
        )
        for copy in range(out.shape[0]):
            out[copy, 0, :, part * dloc:(part + 1) * dloc] = value


def score_kernel(meta, qs, h, hx, out):
    n, heads, wide = qs.shape
    d = wide // 2
    y = meta[3]
    toks = out.shape[1]

    def term(at, rows):
        q = qs[:, :, pl.ds(pl.multiple_of(at * d, d), d)].reshape(n * heads, d)
        hi, lo = split(q)
        both = nt(jnp.concatenate([hi, lo], axis=0), rows)
        return both[:n * heads] + both[n * heads:]

    mine = h[pl.ds(pl.multiple_of(y * toks, toks), toks), :]
    out[...] = term(y, mine) + term(1 - y, hx[...])


def mix_kernel(meta, left, right, h, hx, out):
    n, heads, wide = out.shape
    d = (wide - HD) // 2
    y = meta[3]
    rows, toks = left.shape
    s = (left[...] + right[...]) * (HD ** -0.5)
    top = jnp.max(s, axis=1, keepdims=True)
    weights = jnp.exp(s - top)
    total = jnp.sum(weights, axis=1, keepdims=True)
    hi, lo = split(weights)
    both = jnp.concatenate([hi, lo], axis=0)

    def term(at, values):
        mixed = nn(both, values)
        mixed = (mixed[:rows] + mixed[rows:]).reshape(n, heads, d)
        out[:, :, pl.ds(pl.multiple_of(at * d, d), d)] = mixed

    term(y, h[pl.ds(pl.multiple_of(y * toks, toks), toks), :])
    term(1 - y, hx[...])
    lane = lax.broadcasted_iota(jnp.int32, (rows, HD), 1)
    tail = jnp.where(lane == 0, top, total)
    out[:, :, 2 * d:] = tail.reshape(n, heads, HD)


def value_kernel(meta, assign, got, mixed, w_low, w_high, out, acc, top_ref, total_ref):
    step = pl.program_id(0)
    heads, wide = mixed.shape[2], mixed.shape[3]
    d = (wide - HD) // 2
    tops = [mixed[y, 0, :, 2 * d:2 * d + 1] for y in range(2)]

    @pl.when(step == 0)
    def _():
        own_score, own_v = own_of(got[source(meta, assign)].astype(F32))
        top = jnp.maximum(jnp.maximum(tops[0], tops[1]), own_score)
        own_weight = jnp.exp(own_score - top)
        total = own_weight
        for y in range(2):
            total = total + jnp.exp(tops[y] - top) * mixed[y, 0, :, 2 * d + 1:2 * d + 2]
        acc[0:heads] = own_weight.astype(BF16).astype(F32) * own_v
        acc[heads:] = jnp.zeros((heads, HD), F32)
        top_ref[...] = jnp.broadcast_to(top, top_ref.shape)
        total_ref[...] = jnp.broadcast_to(total, total_ref.shape)

    top = top_ref[:, 0:1]
    both = jnp.exp(tops[0] - top) * mixed[0, 0, :, :2 * d] + jnp.exp(tops[1] - top) * mixed[1, 0, :, :2 * d]
    hi, lo = split(both)
    both = jnp.concatenate([hi, lo], axis=0)
    odd = gather_t(128, 256, 1)
    for part, w in enumerate((w_low, w_high)):
        half = both[:, part * d:(part + 1) * d]
        blocks = d // 128
        tall = jnp.concatenate([half[:, b * 128:(b + 1) * 128] for b in range(blocks)], axis=0)
        spaced = nn(tall, odd).astype(BF16)
        flat = jnp.concatenate([spaced[b * 16:(b + 1) * 16] for b in range(blocks)], axis=1)
        acc[...] += nn(flat, w[...])

    @pl.when(step == pl.num_programs(0) - 1)
    def _():
        done = (acc[0:heads] + acc[heads:]) / total_ref[...]
        for j in range(out.shape[0]):
            out[j] = done


def resident_kernel(first, lengths, query, own, kv, out):
    j = pl.program_id(0) + first
    live = lengths[j]
    rows = query.shape[0]
    wide = query[...].astype(F32)
    pairs = own[...].astype(F32)
    row = wide[0:1]
    ok = pairs[0:1]
    ov = pairs[1:2]
    for r in range(1, rows):
        row = jnp.where(j == r, wide[r:r + 1], row)
        ok = jnp.where(j == r, pairs[2 * r:2 * r + 1], ok)
        ov = jnp.where(j == r, pairs[2 * r + 1:2 * r + 2], ov)
    q = heads_of(row, query.shape[1] // HD)
    own_score = jnp.sum(q * ok, axis=1, keepdims=True) * (HD ** -0.5)
    s = nt(q.astype(BF16), kv[0]) * (HD ** -0.5)
    at = lax.broadcasted_iota(jnp.int32, s.shape, 1)
    valid = (at < 2 * live) & (at % 2 == 0)
    s = jnp.where(valid, s, NEG)
    top = jnp.maximum(jnp.max(s, axis=1, keepdims=True), own_score)
    weights = jnp.where(valid, jnp.exp(s - top), 0.0)
    own_weight = jnp.exp(own_score - top)
    total = jnp.sum(weights, axis=1, keepdims=True) + own_weight
    shifted = pltpu.roll(weights, 1, 1).astype(BF16)
    mixed = nn(shifted, kv[0]) + own_weight.astype(BF16).astype(F32) * ov
    out[0] = mixed / total


def merge_kernel(meta, assign, got, *refs):
    out = refs[-1]
    other, g = 1 - meta[0], meta[1]
    n = assign.shape[1]
    here = [part[k] for part in refs[:-1] for k in range(part.shape[0])]
    rows = []
    for j, value in enumerate(here):
        for i in range(n):
            value = jnp.where(assign[other, i] == g * len(here) + j, got[other * n + i], value)
        rows.append(jnp.concatenate([value[h:h + 1] for h in range(value.shape[0])], axis=1))
    out[...] = jnp.concatenate(rows, axis=0).astype(BF16)


SMEM = pl.BlockSpec(memory_space=pltpu.SMEM)
VMEM = pl.BlockSpec(memory_space=pltpu.VMEM)
MIB = 1024 * 1024


def shaped(shape, dtype):
    return jax.ShapeDtypeStruct(shape, dtype)


def call(kernel, limit, **kw):
    return pl.pallas_call(
        kernel, compiler_params=pltpu.CompilerParams(vmem_limit_bytes=limit * MIB), **kw
    )


def per_device(hidden, w_kv, cache, query, new_kv, lengths, assign):
    h = hidden[0]
    plen, dloc = h.shape
    rows, cap = cache.shape[1], cache.shape[2]
    heads = query.shape[2] // HD
    n_tp = lax.axis_size("tp")
    n_z = n_tp // 2
    n_all = 2 * lax.axis_size("dp")
    toks = plen // 2
    y = lax.axis_index("tp") // n_z
    meta = jnp.stack([lax.axis_index("pool"), lax.axis_index("dp"), rows, y]).astype(jnp.int32)
    w = w_kv.reshape(w_kv.shape[0] * 2, HD)
    kv = cache.reshape(rows, cap * 2, HD)
    q_rows = query[0]
    own = new_kv[0].reshape(rows * 2, HD)

    across = [(i, (i + n_z) % n_tp) for i in range(n_tp)]
    theirs = lax.dynamic_slice_in_dim(h, (1 - y) * toks, toks, 0)
    hx = lax.ppermute(theirs, "tp", across)

    sent = call(
        send_kernel,
        56,
        out_shape=shaped((n_all, 16, HD), BF16),
        in_specs=[SMEM, SMEM, VMEM, VMEM],
        out_specs=VMEM,
        name="send",
    )(meta, assign, q_rows, own)
    got = lax.all_to_all(sent, ("pool", "dp"), 0, 0, tiled=True)

    w_low = pl.BlockSpec((2 * dloc, HD), lambda i: (i, 0))
    w_high = pl.BlockSpec((2 * dloc, HD), lambda i: (i + n_z, 0))
    folded = call(
        fold_kernel,
        56,
        grid=(n_z,),
        out_shape=shaped((2, n_z, heads, 2 * dloc), F32),
        in_specs=[SMEM, SMEM, VMEM, w_low, w_high],
        out_specs=pl.BlockSpec((2, 1, heads, 2 * dloc), lambda i: (0, i, 0, 0)),
        name="fold",
    )(meta, assign, got, w, w)
    folded = folded.reshape(n_tp, heads, 2 * dloc)
    folded = lax.all_to_all(folded, "tp", 0, 0, tiled=True)

    score = call(
        score_kernel,
        24,
        out_shape=shaped((n_tp * heads, toks), F32),
        in_specs=[SMEM, VMEM, VMEM, VMEM],
        out_specs=VMEM,
        name="score",
    )(meta, folded, h, hx)
    near = [(i, i ^ 1) for i in range(n_tp)]
    far = [(i, i ^ 2) for i in range(n_tp)]
    score = score + lax.ppermute(score, "tp", near)
    twin = lax.ppermute(score, "tp", far)

    halves = []
    for first in range(0, rows, 2):
        halves.append(
            call(
                functools.partial(resident_kernel, first),
                24,
                grid=(2,),
                out_shape=shaped((2, heads, HD), F32),
                in_specs=[
                    SMEM,
                    VMEM,
                    VMEM,
                    pl.BlockSpec((1, cap * 2, HD), lambda i, first=first: (i + first, 0, 0)),
                ],
                out_specs=pl.BlockSpec((1, heads, HD), lambda i: (i, 0, 0)),
                name="resident",
                cost_estimate=pl.CostEstimate(
                    flops=2 * 2 * 16 * cap * 2 * HD * 2, bytes_accessed=2 * cap * 2 * HD * 2, transcendentals=0
                ),
            )(lengths[0], q_rows, own, kv)
        )

    mixed = call(
        mix_kernel,
        24,
        out_shape=shaped((n_tp, heads, 2 * dloc + HD), F32),
        in_specs=[SMEM, VMEM, VMEM, VMEM, VMEM],
        out_specs=VMEM,
        name="mix",
    )(meta, score, twin, h, hx)
    mixed = lax.all_to_all(mixed, "tp", 0, 0, tiled=True)

    done = call(
        value_kernel,
        24,
        grid=(n_z,),
        out_shape=shaped((n_all, heads, HD), F32),
        in_specs=[
            SMEM,
            SMEM,
            VMEM,
            pl.BlockSpec((2, 1, heads, 2 * dloc + HD), lambda i: (0, i, 0, 0)),
            w_low,
            w_high,
        ],
        out_specs=VMEM,
        scratch_shapes=[
            pltpu.VMEM((2 * heads, HD), F32),
            pltpu.VMEM((heads, HD), F32),
            pltpu.VMEM((heads, HD), F32),
        ],
        name="value",
    )(meta, assign, got, mixed.reshape(2, n_z, heads, 2 * dloc + HD), w, w)
    done = lax.all_to_all(done, ("pool", "dp"), 0, 0, tiled=True)

    merged = call(
        merge_kernel,
        56,
        out_shape=shaped((rows, heads * HD), BF16),
        in_specs=[SMEM, SMEM] + [VMEM] * (1 + len(halves)),
        out_specs=VMEM,
        name="merge",
    )(meta, assign, done, *halves)
    return merged[None]


def solution(mesh):
    placed = (
        P("pool", "dp", "tp"),
        P(None, None, "tp"),
        P("pool", "dp", None, None, "tp"),
        P("pool", "dp", "tp"),
        P("pool", "dp", None, "tp"),
        P("pool", "dp"),
        P(),
    )
    return jax.shard_map(
        per_device, mesh=mesh, in_specs=placed, out_specs=P("pool", "dp", "tp"), check_vma=False
    )
```

```python
import functools

import jax
import jax.numpy as jnp
from jax import lax
from jax.experimental import pallas as pl
from jax.experimental.pallas import tpu as pltpu
from jax.sharding import PartitionSpec as P

HD = 128
F32 = jnp.float32
BF16 = jnp.bfloat16
NEG = -1e30


def nt(a, b):
    return lax.dot_general(a, b, (((1,), (1,)), ((), ())), preferred_element_type=F32)


def nn(a, b):
    return jnp.dot(a, b, preferred_element_type=F32)


def split(x):
    hi = x.astype(BF16)
    lo = (x - hi.astype(F32)).astype(BF16)
    return hi, lo


def heads_of(row, groups):
    return jnp.concatenate([row[:, h * HD:(h + 1) * HD] for h in range(groups)], axis=0)


def spread(rows, cols, odd):
    r = lax.broadcasted_iota(jnp.int32, (rows, cols), 0)
    c = lax.broadcasted_iota(jnp.int32, (rows, cols), 1)
    return jnp.where(r == 2 * c + odd, 1.0, 0.0).astype(F32).astype(BF16)


def gather_t(rows, cols, odd):
    r = lax.broadcasted_iota(jnp.int32, (rows, cols), 0)
    c = lax.broadcasted_iota(jnp.int32, (rows, cols), 1)
    return jnp.where(c == 2 * r + odd, 1.0, 0.0).astype(F32).astype(BF16)


def own_of(packed):
    q = packed[0:8]
    k = packed[8:9]
    v = packed[9:10]
    return jnp.sum(q * k, axis=1, keepdims=True) * (HD ** -0.5), v


def send_kernel(assign, query, own, out, pick, mask):
    me, g = lax.axis_index("pool"), lax.axis_index("dp")
    rows = query.shape[0]
    n = assign.shape[1]
    q = query[...].astype(F32)
    kv = own[...].astype(F32)
    packed = []
    for j in range(rows):
        mine = heads_of(q[j:j + 1], q.shape[1] // HD)
        pad = jnp.zeros((16 - mine.shape[0] - 2, HD), F32)
        packed.append(jnp.concatenate([mine, kv[2 * j:2 * j + 2], pad], axis=0))
    for i in range(n):
        at = assign[1 - me, i] - g * rows
        value = packed[0]
        for j in range(1, rows):
            value = jnp.where(at == j, packed[j], value)
        value = value.astype(BF16)
        out[i] = value
        out[n + i] = value
    source = (1 - me) * n + assign[me, g] // rows
    slot = lax.broadcasted_iota(jnp.int32, pick.shape, 0)
    pick[...] = jnp.where(slot == source, 1.0, 0.0)
    slots = 2 * n
    slot = lax.broadcasted_iota(jnp.int32, mask.shape, 0)
    chosen = jnp.zeros(mask.shape, F32)
    for i in range(n):
        at = assign[1 - me, i] - g * rows
        target = jnp.where((at >= 0) & (at < rows), at * slots + (1 - me) * n + i, -1)
        chosen = jnp.where(slot == target, 1.0, chosen)
    mask[...] = chosen


def stage_kernel(odd, w, *refs):
    out = refs[-1]
    pick = gather_t(128, 256, odd)
    for b in range(out.shape[0] // 128):
        out[b * 128:(b + 1) * 128] = nn(pick, w[b * 256:(b + 1) * 256]).astype(BF16)


def fold_kernel(got, pick, w, out, mine):
    row = jnp.zeros(mine.shape, F32)
    for j in range(got.shape[0]):
        row = jnp.where(pick[j:j + 1] > 0.5, got[j].astype(F32), row)
    mine[...] = row
    d = out.shape[2]
    wide = nt(row[0:8].astype(BF16), w[...])
    for j in range(out.shape[0]):
        out[j] = wide[:, j * d:(j + 1) * d]


def score_kernel(qs, h, out):
    n, heads, d = qs.shape
    hi, lo = split(qs[...].reshape(n * heads, d))
    both = nt(jnp.concatenate([hi, lo], axis=0), h[...])
    out[...] = both[:n * heads] + both[n * heads:]


def mix_kernel(left, right, mine, h, first, second, values, out, scale_out, own_out, top_ref, total_ref):
    n, heads, d = out.shape
    t = lax.axis_index("tp")
    s = (left[...] + right[...]) * (HD ** -0.5)
    top = jnp.max(s, axis=1, keepdims=True)
    weights = jnp.exp(s - top)
    total = jnp.sum(weights, axis=1, keepdims=True)
    out[...] = nn(weights.astype(BF16), h[...]).reshape(n, heads, d)
    top_ref[...] = jnp.broadcast_to(top, top_ref.shape)
    total_ref[...] = jnp.broadcast_to(total, total_ref.shape)
    at = pl.ds(pl.multiple_of(t * heads, heads), heads)
    own_score, own_v = own_of(mine[...])
    here = top_ref[at, :]
    both = jnp.maximum(here, own_score)
    own_weight = jnp.exp(own_score - both)
    shrink = jnp.exp(here - both)
    whole = shrink * total_ref[at, :] + own_weight
    scale_out[...] = shrink / whole
    own_out[...] = own_weight.astype(BF16).astype(F32) * own_v / whole


def value_kernel(mixed, w, scale, own, out):
    n, heads, d = mixed.shape
    acc = jnp.zeros((2 * heads, HD), F32)
    for j in range(n):
        hi, lo = split(mixed[j])
        acc = acc + nn(jnp.concatenate([hi, lo], axis=0), w[d * j:d * (j + 1), :])
    done = (acc[:heads] + acc[heads:]) * scale[...] + own[...]
    for j in range(out.shape[0]):
        out[j] = done


def resident_kernel(first, lengths, query, own, kv, after, out):
    j = pl.program_id(0) + first
    live = lengths[j]
    rows = query.shape[0]
    wide = query[...].astype(F32)
    pairs = own[...].astype(F32)
    row = wide[0:1]
    ok = pairs[0:1]
    ov = pairs[1:2]
    for r in range(1, rows):
        row = jnp.where(j == r, wide[r:r + 1], row)
        ok = jnp.where(j == r, pairs[2 * r:2 * r + 1], ok)
        ov = jnp.where(j == r, pairs[2 * r + 1:2 * r + 2], ov)
    q = heads_of(row, query.shape[1] // HD)
    own_score = jnp.sum(q * ok, axis=1, keepdims=True) * (HD ** -0.5)
    s = nt(q.astype(BF16), kv[0]) * (HD ** -0.5)
    at = lax.broadcasted_iota(jnp.int32, s.shape, 1)
    valid = (at < 2 * live) & (at % 2 == 0)
    s = jnp.where(valid, s, NEG)
    top = jnp.maximum(jnp.max(s, axis=1, keepdims=True), own_score)
    weights = jnp.where(valid, jnp.exp(s - top), 0.0)
    own_weight = jnp.exp(own_score - top)
    total = jnp.sum(weights, axis=1, keepdims=True) + own_weight
    shifted = pltpu.roll(weights, 1, 1).astype(BF16)
    mixed = nn(shifted, kv[0]) + own_weight.astype(BF16).astype(F32) * ov
    out[0] = mixed / total


def merge_kernel(mask, got, *refs):
    out = refs[-1]
    n = got.shape[0]
    here = [part[k] for part in refs[:-1] for k in range(part.shape[0])]
    rows = []
    for j, value in enumerate(here):
        for i in range(n):
            value = jnp.where(mask[j * n + i:j * n + i + 1] > 0.5, got[i], value)
        rows.append(jnp.concatenate([value[h:h + 1] for h in range(value.shape[0])], axis=1))
    out[...] = jnp.concatenate(rows, axis=0).astype(BF16)


SMEM = pl.BlockSpec(memory_space=pltpu.SMEM)
VMEM = pl.BlockSpec(memory_space=pltpu.VMEM)
ANY = pl.BlockSpec(memory_space=pl.ANY)
MIB = 1024 * 1024


def shaped(shape, dtype):
    return jax.ShapeDtypeStruct(shape, dtype)


def call(kernel, limit, **kw):
    return pl.pallas_call(
        kernel, compiler_params=pltpu.CompilerParams(vmem_limit_bytes=limit * MIB), **kw
    )


def per_device(hidden, w_kv, cache, query, new_kv, lengths, assign):
    h = hidden[0]
    plen, dloc = h.shape
    rows, cap = cache.shape[1], cache.shape[2]
    heads = query.shape[2] // HD
    n_tp = lax.axis_size("tp")
    n_dp = lax.axis_size("dp")
    n_all = 2 * n_dp
    w = w_kv.reshape(w_kv.shape[0] * 2, HD)
    kv = cache.reshape(rows, cap * 2, HD)
    q_rows = query[0]
    own = new_kv[0].reshape(rows * 2, HD)

    sent, pick, mask = call(
        send_kernel,
        56,
        out_shape=[
            shaped((n_all, 16, HD), BF16),
            shaped((n_all, HD), F32),
            shaped((rows * n_all, HD), F32),
        ],
        in_specs=[SMEM, VMEM, VMEM],
        out_specs=[VMEM, VMEM, VMEM],
        name="send",
    )(assign, q_rows, own)
    def stage(odd, *after):
        return call(
            functools.partial(stage_kernel, odd),
            24,
            out_shape=shaped((w_kv.shape[0], HD), BF16),
            in_specs=[VMEM] + [ANY] * len(after),
            out_specs=VMEM,
            name="stage",
            cost_estimate=pl.CostEstimate(
                flops=4 * w.size * HD, bytes_accessed=3 * w.size, transcendentals=0
            ),
        )(w, *after)

    keys = stage(0)
    got = lax.all_to_all(sent, ("pool", "dp"), 0, 0, tiled=True)
    h, got = lax.optimization_barrier((h, got))

    folded, mine = call(
        fold_kernel,
        24,
        out_shape=[shaped((n_tp, heads, dloc), F32), shaped((16, HD), F32)],
        in_specs=[VMEM, VMEM, VMEM],
        out_specs=[VMEM, VMEM],
        name="fold",
    )(got, pick, keys)
    folded = lax.all_to_all(folded, "tp", 0, 0, tiled=True)

    score = call(
        score_kernel,
        24,
        out_shape=shaped((n_tp * heads, plen), F32),
        in_specs=[VMEM, VMEM],
        out_specs=VMEM,
        name="score",
    )(folded, h)

    def resident(first, after):
        return call(
            functools.partial(resident_kernel, first),
            24,
            grid=(2,),
            out_shape=shaped((2, heads, HD), F32),
            in_specs=[
                SMEM,
                VMEM,
                VMEM,
                pl.BlockSpec((1, cap * 2, HD), lambda i: (i + first, 0, 0)),
                ANY,
            ],
            out_specs=pl.BlockSpec((1, heads, HD), lambda i: (i, 0, 0)),
            name="resident",
            cost_estimate=pl.CostEstimate(
                flops=2 * 2 * 16 * cap * 2 * HD * 2, bytes_accessed=2 * cap * 2 * HD * 2, transcendentals=0
            ),
        )(lengths[0], q_rows, own, kv, after)

    def exchange(x, even, odd):
        pairs = []
        for g in range(n_dp):
            for t in range(n_tp):
                pairs.append((g * n_tp + t, g * n_tp + (even, odd)[g % 2](t)))
        return lax.ppermute(x, ("dp", "tp"), pairs)

    n_z = n_tp // 2

    def far(t):
        return (t + n_z) % n_tp

    def up(t):
        return t ^ 1

    def down(t):
        return t // n_z * n_z + n_z - 1 - t % n_z

    values = stage(1, score)
    first = resident(0, score)
    score = score + exchange(score, far, down)
    second = resident(2, score)
    score = score + exchange(score, up, far)
    twin = exchange(score, down, up)

    mixed, scale, own_part = call(
        mix_kernel,
        24,
        out_shape=[shaped((n_tp, heads, dloc), F32), shaped((heads, HD), F32), shaped((heads, HD), F32)],
        in_specs=[VMEM, VMEM, VMEM, VMEM, ANY, ANY, ANY],
        out_specs=[VMEM, VMEM, VMEM],
        scratch_shapes=[pltpu.VMEM((n_tp * heads, HD), F32), pltpu.VMEM((n_tp * heads, HD), F32)],
        name="mix",
    )(score, twin, mine, h, first, second, values)
    mixed = lax.all_to_all(mixed, "tp", 0, 0, tiled=True)

    done = call(
        value_kernel,
        24,
        out_shape=shaped((n_all, heads, HD), F32),
        in_specs=[VMEM, VMEM, VMEM, VMEM],
        out_specs=VMEM,
        name="value",
    )(mixed, values, scale, own_part)
    done = lax.all_to_all(done, ("pool", "dp"), 0, 0, tiled=True)

    merged = call(
        merge_kernel,
        24,
        out_shape=shaped((rows, heads * HD), BF16),
        in_specs=[VMEM, VMEM, VMEM, VMEM],
        out_specs=VMEM,
        name="merge",
    )(mask, done, first, second)
    return merged[None]


def solution(mesh):
    placed = (
        P("pool", "dp", "tp"),
        P(None, None, "tp"),
        P("pool", "dp", None, None, "tp"),
        P("pool", "dp", "tp"),
        P("pool", "dp", None, "tp"),
        P("pool", "dp"),
        P(),
    )
    return jax.shard_map(
        per_device, mesh=mesh, in_specs=placed, out_specs=P("pool", "dp", "tp"), check_vma=False
    )
```
